32 devices in a mesh: groups: 2 (over y), blk: 4 (over x, core), fetch: 4 (over z).
Axes of the slice: x: 2, y: 2, z: 4, core: 2. Of those that a mesh axis runs over, the one named last changes fastest.
Arguments:
- amplitudes: bfloat16 [3584, 3072], P(('groups', 'fetch'), 'blk'), parts along dimension 0, may hold values from -6 to 6
- integrals: bfloat16 [8, 12, 256, 1024], P(('groups', 'blk'), 'fetch'), parts along dimension 0, may hold values from -0.15625 to 0.15625
- tile_ids: int32 [8, 12], P(('groups', 'blk')), parts along dimension 0, may hold values from -1 to 11, as said below
Outputs:
- ladder: bfloat16 [3584, 4096], P(('groups', 'fetch'), 'blk'), parts along dimension 0
The draws below stay inside these ranges and needn't reach their ends.
There are 2 independent parts, one for each index of `groups`. The reference program is written for one: setup_inputs(seed, part) draws one part's arguments, and reference() takes and returns one part's arrays. A program takes and returns all parts, laid end to end along the dimension named above; each array names one. Nothing has to cross between parts.
Inputs may be any that keep to these rules, and one draw needn't show every extreme that they name: `tile_ids`: row r gives 4 owners in turn, 3 slots each: an owner's tiles first, then -1 in its empty slots. Every owner holds at least one tile, in every row some owner holds 3, and the tiles named in one row are distinct.
All inputs are finite; a program needn't handle non-finite values.
Results may differ from the reference program's by a relative error of at most 0.001.
Values may be sent and summed in bfloat16 or wider, within the bound.
A program may use at most 128 MiB of HBM per device.

```python
import jax
import jax.numpy as jnp
from jax import lax

TILE = 256
COLS = 1024
SLOTS = 3
IJ = 1792
NTILE = 12
N_BLK = 4
N_FETCH = 4


def draw_tile_ids(key, part):
    key = jax.random.fold_in(key, 11)

    def one_block(row_key):
        count_key, full_key, order_key = jax.random.split(row_key, 3)
        counts = jax.random.randint(count_key, (N_FETCH,), 1, SLOTS + 1)
        fullest = jax.random.randint(full_key, (), 0, N_FETCH)
        counts = jnp.where(jnp.arange(N_FETCH) == fullest, SLOTS, counts)
        ordering = jax.random.permutation(order_key, NTILE)
        offsets = jnp.cumsum(counts) - counts
        slot_range = jnp.arange(SLOTS)
        position = jnp.minimum(offsets[:, None] + slot_range[None, :], NTILE - 1)
        chosen = ordering[position]
        return jnp.where(slot_range[None, :] < counts[:, None], chosen, -1).reshape(-1)
    return jax.vmap(one_block)(jax.random.split(key, N_BLK)).astype(jnp.int32)


def levels(rng, dims, shards, least, top_value):
    loudness, own = 1.0, jax.random.fold_in(rng, 6)
    for axis_at, parts in shards:
        heights = jnp.exp(jax.random.uniform(jax.random.fold_in(own, axis_at), (parts,), jnp.float32, least / len(shards), top_value / len(shards)))
        loudness = loudness * jnp.repeat(heights, dims[axis_at] // parts).reshape([-1 if axis == axis_at else 1 for axis in range(len(dims))])
    return loudness


def normal_values(rng, dims, width, reach, cuts=(), kind=jnp.bfloat16):
    result = jax.random.normal(rng, dims, jnp.float32) * width
    if len(cuts) > 0:
        result = levels(rng, dims, cuts, -0.22, 0.18) * result
    return jnp.clip(result, min=-reach, max=reach).astype(kind)


def setup_inputs(seed: int = 0, part: int = 0) -> dict:
    key_list = jax.random.split(jax.random.key(seed), 4)
    part_splits = jax.random.split(jax.random.fold_in(key_list[3], part), 4)
    amplitudes = normal_values(part_splits[0], (IJ, NTILE * TILE), 1.0, 6.0, ((0, 4), (1, 4)))
    integrals = normal_values(part_splits[1], (N_BLK, N_FETCH * SLOTS, TILE, COLS), (N_FETCH * SLOTS * TILE // 2) ** -0.5, 0.15625, ((0, 4), (1, 4)))
    tile_ids = draw_tile_ids(jax.random.fold_in(jax.random.fold_in(key_list[3], part), 71), part)
    return dict(amplitudes=amplitudes, integrals=integrals, tile_ids=tile_ids)


def reference(amplitudes, integrals, tile_ids):
    widened = amplitudes.astype(jnp.float32)
    tile_range = jnp.arange(NTILE, dtype=jnp.int32)

    def column_block(operands):
        block_tiles, block_ids = operands
        selector = (block_ids[None, :] == tile_range[:, None]).astype(jnp.float32)
        dense_rows = jnp.einsum("ks,stc->ktc", selector, block_tiles.astype(jnp.float32), precision=lax.Precision.HIGHEST)
        dense_rows = dense_rows.reshape(NTILE * TILE, COLS)
        product = jnp.dot(widened, dense_rows, precision=lax.Precision.HIGHEST)
        return product.astype(jnp.bfloat16)

    blocks = lax.map(column_block, (integrals, tile_ids))
    return jnp.transpose(blocks, (1, 0, 2)).reshape(IJ, N_BLK * COLS)
```

```python
import functools

import jax
import jax.numpy as jnp
from jax import lax
from jax.experimental import pallas as pl
from jax.experimental.pallas import tpu as pltpu
from jax.sharding import PartitionSpec as P

CORES = 2
CHUNKS = 4
MESH = pl.DeviceIdType.MESH


def kernel(
    n, chips, lead,
    ids_ref, a_ref, b_ref, out_ref,
    abuf, aout, bbuf, acc, acc2, obuf, rbuf,
    local_sem, a_send, a_recv, s_send, s_recv, o_send, o_recv,
    p_send, m_send, b_recv, r_sem,
):
    g = lax.axis_index("groups")
    b = lax.axis_index("blk")
    f = lax.axis_index("fetch")
    x, core = lax.div(b, CORES), lax.rem(b, CORES)
    sibling = b + 1 - 2 * core
    slots, tile, columns = b_ref.shape[1:]
    step_rows = tile // CHUNKS
    per_group = a_ref.shape[1] // tile

    low = f < n // 2
    way = jnp.where(low, 1, -1)
    far_hops = jnp.where(low, n - 1 - f, f)
    near_hops = n - 1 - far_hops
    is_end = near_hops == 0
    is_helper = near_hops == 1
    far_side = (g, b, jnp.clip(f + way, 0, n - 1))
    near_side = (g, b, jnp.clip(f - way, 0, n - 1))
    has_near = near_hops > 0

    def mate(hop):
        return lax.rem(x + hop, chips) * CORES + core

    barrier = pltpu.get_barrier_semaphore()
    for hop in range(1, chips):
        pl.semaphore_signal(barrier, inc=1, device_id=(g, mate(hop), f), device_id_type=MESH)
    pl.semaphore_signal(barrier, inc=1, device_id=(g, sibling, f), device_id_type=MESH)
    pl.semaphore_signal(barrier, inc=1, device_id=far_side, device_id_type=MESH)

    @pl.when(has_near)
    def _():
        pl.semaphore_signal(barrier, inc=1, device_id=near_side, device_id_type=MESH)

    own_a = [
        pltpu.make_async_copy(
            a_ref.at[:, pl.ds(k * tile, tile)], abuf.at[b * per_group + k], local_sem.at[1 + k]
        )
        for k in range(per_group)
    ]
    own_b = pltpu.make_async_copy(b_ref.at[0], bbuf.at[f], local_sem.at[0])
    for copy in own_a:
        copy.start()
    own_b.start()
    pl.semaphore_wait(barrier, chips + 1 + jnp.where(has_near, 1, 0))

    def remote(src, dst, send, recv, device):
        return pltpu.make_async_remote_copy(
            src_ref=src, dst_ref=dst, send_sem=send, recv_sem=recv,
            device_id=device, device_id_type=MESH,
        )

    def b_copy(owner, slot, chunk, device, send, width, src=None):
        rows = pl.ds(chunk * step_rows, step_rows)
        piece = bbuf.at[owner, slot, rows, pl.ds(0, width)]
        source = piece if src is None else src.at[0, slot, rows, pl.ds(0, width)]
        return remote(source, piece, send.at[owner, slot, chunk], b_recv.at[owner, slot, chunk], device)

    def to_far(owner, slot, chunk, src=None):
        return b_copy(owner, slot, chunk, far_side, p_send, columns, src)

    def near_each(owner, slot, src, action):
        @pl.when(is_helper)
        def _():
            for chunk in range(CHUNKS):
                action(b_copy(owner, slot, chunk, near_side, m_send, lead, src))

        @pl.when(near_hops > 1)
        def _():
            for chunk in range(CHUNKS):
                action(b_copy(owner, slot, chunk, near_side, m_send, columns, src))

    def a_group(buffer, owner):
        return buffer.at[pl.ds(owner * per_group, per_group)]

    def a_mate(buffer, hop, base):
        part = a_group(buffer, b)
        return remote(part, part, a_send.at[base, hop], a_recv.at[base, hop], (g, mate(hop), f))

    def a_sib(buffer, hop, base):
        part = a_group(buffer, lax.rem(x + chips - hop, chips) * CORES + core)
        return remote(part, part, s_send.at[base, hop], s_recv.at[base, hop], (g, sibling, f))

    for copy in own_a:
        copy.wait()
    for hop in range(1, chips):
        a_mate(abuf, hop, 0).start()
    a_sib(abuf, 0, 0).start()

    a_help = remote(a_group(abuf, b), a_group(aout, b), o_send.at[0], o_recv.at[0], far_side)

    @pl.when(is_end)
    def _():
        a_help.start()

    for slot in range(slots):
        for chunk in range(CHUNKS):
            to_far(f, slot, chunk, b_ref).start()
        near_each(f, slot, b_ref, lambda copy: copy.start())

        if slot == 0:
            @pl.when(is_end)
            def _():
                a_help.wait_send()

    own_b.wait()
    for hop in range(1, chips):
        a_mate(abuf, hop, 0).wait_recv()
        a_sib(abuf, hop, 0).start()
    for hop in range(chips):
        a_sib(abuf, hop, 0).wait_recv()

    def a_tile(buffer, owner, slot):
        name = ids_ref[0, owner * slots + slot]
        empty = lax.shift_right_arithmetic(name, 31)
        value = buffer[name - empty]
        return value * (1 + empty).astype(jnp.float32).astype(value.dtype)

    def add(owner, slot):
        piece = a_tile(abuf, owner, slot)
        acc[:, :lead] += jnp.dot(piece, bbuf[owner, slot, :, :lead], preferred_element_type=jnp.float32)

        @pl.when(jnp.logical_not(is_end))
        def _():
            acc[:, lead:] += jnp.dot(piece, bbuf[owner, slot, :, lead:], preferred_element_type=jnp.float32)

    def add_help(owner, slot):
        piece = a_tile(aout, owner, slot)
        acc2[...] += jnp.dot(piece, bbuf[owner, slot, :, lead:], preferred_element_type=jnp.float32)

    acc[...] = jnp.zeros_like(acc)
    acc2[...] = jnp.zeros_like(acc2)

    def own_slot(slot, carry):
        add(f, slot)
        return carry

    lax.fori_loop(0, slots, own_slot, 0)

    last_owner = f + way * far_hops

    def step(j, carry):
        @pl.when(is_helper & (j == 2))
        def _():
            a_help.wait_recv()
            for hop in range(1, chips):
                a_mate(aout, hop, 1).start()
            a_sib(aout, 0, 1).start()

        @pl.when(is_helper & (j == 4))
        def _():
            for hop in range(1, chips):
                a_mate(aout, hop, 1).wait_recv()
                a_sib(aout, hop, 1).start()

        final = j == slots * far_hops - 1

        @pl.when(is_helper & final)
        def _():
            for hop in range(chips):
                a_sib(aout, hop, 1).wait_recv()

            def one(index, carry):
                owner, slot = lax.div(index, slots), lax.rem(index, slots)

                @pl.when(jnp.logical_not((owner == last_owner) & (slot == slots - 1)))
                def _():
                    add_help(owner, slot)
                return carry

            lax.fori_loop(0, n * slots, one, 0)

        @pl.when(j < slots * far_hops)
        def _():
            owner = f + way * (1 + lax.div(j, slots))
            slot = lax.rem(j, slots)

            @pl.when(is_end)
            def _():
                for chunk in range(CHUNKS):
                    b_copy(owner, slot, chunk, far_side, m_send, lead).wait_recv()

            @pl.when(is_helper)
            def _():
                for chunk in range(CHUNKS):
                    b_copy(owner, slot, chunk, far_side, m_send, columns).wait_recv()
                    b_copy(owner, slot, chunk, near_side, m_send, lead).start()

            @pl.when(near_hops > 1)
            def _():
                for chunk in range(CHUNKS):
                    b_copy(owner, slot, chunk, far_side, m_send, columns).wait_recv()
                    b_copy(owner, slot, chunk, near_side, m_send, columns).start()

            @pl.when(is_helper & final)
            def _():
                add_help(owner, slot)
                obuf[...] = acc2[...].astype(obuf.dtype)
                remote(obuf, rbuf, r_sem.at[0], r_sem.at[1], near_side).start()

            add(owner, slot)

        back = j - 1

        @pl.when((back >= 0) & (back < slots * near_hops))
        def _():
            owner = f - way * (1 + lax.div(back, slots))
            slot = lax.rem(back, slots)
            for chunk in range(CHUNKS):
                to_far(owner, slot, chunk).wait_recv()
                to_far(owner, slot, chunk).start()
            add(owner, slot)

        return carry

    lax.fori_loop(0, slots * (n - 1), step, 0)

    out_ref[:, :lead] = acc[:, :lead].astype(out_ref.dtype)
    result = remote(obuf, rbuf, r_sem.at[0], r_sem.at[1], near_side)

    @pl.when(is_end)
    def _():
        result.wait_recv()
        out_ref[:, lead:] = rbuf[...]

    @pl.when(jnp.logical_not(is_end))
    def _():
        out_ref[:, lead:] = acc[:, lead:].astype(out_ref.dtype)

    def far_done(k, carry):
        owner, slot = f - way * lax.div(k, slots), lax.rem(k, slots)
        for chunk in range(CHUNKS):
            to_far(owner, slot, chunk).wait_send()
        return carry

    lax.fori_loop(0, slots * (near_hops + 1), far_done, 0)

    @pl.when(has_near)
    def _():
        def near_done(k, carry):
            owner, slot = f + way * lax.div(k, slots), lax.rem(k, slots)
            near_each(owner, slot, None, lambda copy: copy.wait_send())
            return carry

        lax.fori_loop(0, slots * (far_hops + 1), near_done, 0)

    for hop in range(1, chips):
        a_mate(abuf, hop, 0).wait_send()
    for hop in range(chips):
        a_sib(abuf, hop, 0).wait_send()

    @pl.when(is_helper)
    def _():
        for hop in range(1, chips):
            a_mate(aout, hop, 1).wait_send()
        for hop in range(chips):
            a_sib(aout, hop, 1).wait_send()
        result.wait_send()


def per_device(mesh_shape, amplitudes, integrals, tile_ids):
    n, chips = mesh_shape["fetch"], mesh_shape["blk"] // CORES
    rows, width = amplitudes.shape
    _, slots, tile, columns = integrals.shape
    lead = columns * 5 // 8
    tiles = chips * CORES * width // tile
    bf16, f32, dma = jnp.bfloat16, jnp.float32, pltpu.SemaphoreType.DMA
    return pl.pallas_call(
        functools.partial(kernel, n, chips, lead),
        out_shape=jax.ShapeDtypeStruct((rows, columns), bf16),
        in_specs=[
            pl.BlockSpec(memory_space=pltpu.SMEM),
            pl.BlockSpec(memory_space=pl.ANY),
            pl.BlockSpec(memory_space=pl.ANY),
        ],
        out_specs=pl.BlockSpec(memory_space=pltpu.VMEM),
        scratch_shapes=[
            pltpu.VMEM((tiles, rows, tile), bf16),
            pltpu.VMEM((tiles, rows, tile), bf16),
            pltpu.VMEM((n, slots, tile, columns), bf16),
            pltpu.VMEM((rows, columns), f32),
            pltpu.VMEM((rows, columns - lead), f32),
            pltpu.VMEM((rows, columns - lead), bf16),
            pltpu.VMEM((rows, columns - lead), bf16),
            dma((1 + width // tile,)),
            dma((2, chips)), dma((2, chips)),
            dma((2, chips)), dma((2, chips)),
            dma((1,)), dma((1,)),
            dma((n, slots, CHUNKS)), dma((n, slots, CHUNKS)), dma((n, slots, CHUNKS)),
            dma((2,)),
        ],
        compiler_params=pltpu.CompilerParams(
            collective_id=0, has_side_effects=True, vmem_limit_bytes=56 << 20
        ),
        cost_estimate=pl.CostEstimate(
            flops=2 * rows * n * slots * tile * columns,
            bytes_accessed=4 * rows * columns, transcendentals=0,
        ),
    )(tile_ids, amplitudes, integrals)


def solution(mesh):
    placed = (
        P(("groups", "fetch"), "blk"),
        P(("groups", "blk"), "fetch", None, None),
        P(("groups", "blk"), None),
    )
    return jax.shard_map(
        functools.partial(per_device, dict(mesh.shape)),
        mesh=mesh,
        in_specs=placed,
        out_specs=P(("groups", "fetch"), "blk"),
        check_vma=False,
    )
```

```python
import functools

import jax
import jax.numpy as jnp
from jax import lax
from jax.experimental import pallas as pl
from jax.experimental.pallas import tpu as pltpu
from jax.sharding import PartitionSpec as P

CORES = 2
LAG = 4
MESH = pl.DeviceIdType.MESH


def kernel(
    n, chips, cuts,
    ids_ref, a_ref, b_ref, out_ref,
    abuf, aout, bbuf, acc, acc_first, acc_last, o_first, o_last, r_first, r_last,
    local_sem, a_send, a_recv, s_send, s_recv, o_send, o_recv,
    p_send, m_send, b_recv, r_send, r_recv,
):
    g = lax.axis_index("groups")
    b = lax.axis_index("blk")
    f = lax.axis_index("fetch")
    x, core = lax.div(b, CORES), lax.rem(b, CORES)
    sibling = b + 1 - 2 * core
    slots, tile, columns = b_ref.shape[1:]
    per_group = a_ref.shape[1] // tile
    spans = [slice(0, cuts[0]), slice(cuts[0], cuts[1]), slice(cuts[1], columns)]

    low = f < n // 2
    way = jnp.where(low, 1, -1)
    far_hops = jnp.where(low, n - 1 - f, f)
    near_hops = n - 1 - far_hops
    is_end = near_hops == 0
    is_helper = near_hops == 1
    has_near = near_hops > 0
    far_side = (g, b, jnp.clip(f + way, 0, n - 1))
    near_side = (g, b, jnp.clip(f - way, 0, n - 1))

    def mate(hop):
        return lax.rem(x + hop, chips) * CORES + core

    barrier = pltpu.get_barrier_semaphore()
    for hop in range(1, chips):
        pl.semaphore_signal(barrier, inc=1, device_id=(g, mate(hop), f), device_id_type=MESH)
    pl.semaphore_signal(barrier, inc=1, device_id=(g, sibling, f), device_id_type=MESH)
    pl.semaphore_signal(barrier, inc=1, device_id=far_side, device_id_type=MESH)

    @pl.when(has_near)
    def _():
        pl.semaphore_signal(barrier, inc=1, device_id=near_side, device_id_type=MESH)

    own_a = [
        pltpu.make_async_copy(
            a_ref.at[:, pl.ds(k * tile, tile)], abuf.at[b * per_group + k], local_sem.at[1 + k]
        )
        for k in range(per_group)
    ]
    own_b = pltpu.make_async_copy(b_ref.at[0], bbuf.at[f], local_sem.at[0])
    for copy in own_a:
        copy.start()
    own_b.start()
    for copy in own_a:
        copy.wait()
    pl.semaphore_wait(barrier, chips + 1 + jnp.where(has_near, 1, 0))

    def remote(src, dst, send, recv, device):
        return pltpu.make_async_remote_copy(
            src_ref=src, dst_ref=dst, send_sem=send, recv_sem=recv,
            device_id=device, device_id_type=MESH,
        )

    def b_copy(span, owner, slot, device, send, src=None):
        lanes = pl.ds(spans[span].start, spans[span].stop - spans[span].start)
        piece = bbuf.at[owner, slot, :, lanes]
        source = piece if src is None else src.at[0, slot, :, lanes]
        return remote(source, piece, send.at[owner, slot, span], b_recv.at[owner, slot, span], device)

    def to_far(span, owner, slot, src=None):
        return b_copy(span, owner, slot, far_side, p_send, src)

    def to_near(span, owner, slot, src=None):
        return b_copy(span, owner, slot, near_side, m_send, src)

    def sends_near(span):
        return has_near if span == 1 else near_hops > 1

    def a_group(buffer, owner):
        return buffer.at[pl.ds(owner * per_group, per_group)]

    def a_mate(buffer, hop, base):
        part = a_group(buffer, b)
        return remote(part, part, a_send.at[base, hop], a_recv.at[base, hop], (g, mate(hop), f))

    def a_sib(buffer, hop, base):
        part = a_group(buffer, lax.rem(x + chips - hop, chips) * CORES + core)
        return remote(part, part, s_send.at[base, hop], s_recv.at[base, hop], (g, sibling, f))

    def start_own(span):
        for slot in range(slots):
            to_far(span, f, slot, b_ref).start()

        @pl.when(sends_near(span))
        def _():
            for slot in range(slots):
                to_near(span, f, slot, b_ref).start()

    a_help = remote(a_group(abuf, b), a_group(aout, b), o_send.at[0], o_recv.at[0], far_side)

    @pl.when(is_end)
    def _():
        a_help.start()

    start_own(0)
    for hop in range(1, chips):
        a_mate(abuf, hop, 0).start()
    a_sib(abuf, 0, 0).start()

    @pl.when(jnp.logical_not(is_end))
    def _():
        start_own(1)

    acc[...] = jnp.zeros_like(acc)
    acc_first[...] = jnp.zeros_like(acc_first)
    acc_last[...] = jnp.zeros_like(acc_last)
    own_b.wait()

    def a_tile(buffer, owner, slot):
        name = ids_ref[0, owner * slots + slot]
        empty = lax.shift_right_arithmetic(name, 31)
        value = buffer[name - empty]
        return value * (1 + empty).astype(jnp.float32).astype(value.dtype)

    def add(span, owner, slot):
        part = spans[span]
        acc[:, part] += jnp.dot(
            a_tile(abuf, owner, slot), bbuf[owner, slot, :, part], preferred_element_type=jnp.float32
        )

    def add_help(span, total, owner, slot):
        total[...] += jnp.dot(
            a_tile(aout, owner, slot), bbuf[owner, slot, :, spans[span]],
            preferred_element_type=jnp.float32,
        )

    def item(index, hops, direction):
        tail = index - 2 * slots * hops
        late = tail >= 0
        span = jnp.where(late, 2, lax.rem(lax.div(index, slots), 2))
        distance = 1 + jnp.where(late, lax.div(tail, slots), lax.div(index, 2 * slots))
        return span, f + direction * distance, lax.rem(index, slots)

    def by_span(span, action):
        for which in range(3):
            @pl.when(span == which)
            def _(which=which):
                action(which)

    def far_item(index):
        return item(index, far_hops, way)

    def far_add(index):
        span, owner, slot = far_item(index)

        def one(which):
            if which == 1:
                add(which, owner, slot)
            else:
                pl.when(jnp.logical_not(is_end))(lambda: add(which, owner, slot))

        by_span(span, one)

    first_result = remote(o_first, r_first, r_send.at[0], r_recv.at[0], near_side)
    last_result = remote(o_last, r_last, r_send.at[1], r_recv.at[1], near_side)
    far_items = 3 * slots * far_hops
    near_items = 3 * slots * near_hops
    far_end = f + way * far_hops

    def step(j, carry):
        @pl.when(j == 3)
        def _():
            for hop in range(1, chips):
                a_mate(abuf, hop, 0).wait_recv()
                a_sib(abuf, hop, 0).start()

            @pl.when(is_end)
            def _():
                a_help.wait_send()
                start_own(1)

            @pl.when(is_helper)
            def _():
                a_help.wait_recv()
                for hop in range(1, chips):
                    a_mate(aout, hop, 1).start()
                a_sib(aout, 0, 1).start()

        @pl.when(is_helper & (j == 6))
        def _():
            for hop in range(1, chips):
                a_mate(aout, hop, 1).wait_recv()
                a_sib(aout, hop, 1).start()

        @pl.when(is_helper & (j == 7))
        def _():
            for hop in range(chips):
                a_sib(aout, hop, 1).wait_recv()

        @pl.when(is_helper & (j == far_items - 1))
        def _():
            def one(index, carry):
                owner, slot = lax.div(index, slots), lax.rem(index, slots)

                @pl.when(jnp.logical_not((owner == far_end) & (slot == slots - 1)))
                def _():
                    add_help(2, acc_last, owner, slot)
                return carry

            lax.fori_loop(0, n * slots, one, 0)

        span, owner, slot = far_item(j)

        def arrive(which):
            @pl.when(jnp.logical_not(is_end) if which != 1 else j >= 0)
            def _():
                to_near(which, owner, slot).wait_recv()

            @pl.when(sends_near(which))
            def _():
                to_near(which, owner, slot).start()

        by_span(span, arrive)

        @pl.when(is_helper & (j == far_items - 1))
        def _():
            add_help(2, acc_last, owner, slot)
            o_last[...] = acc_last[...].astype(o_last.dtype)
            last_result.start()

        back = j - LAG
        near = (back >= 0) & (back < near_items)
        near_span, near_owner, near_slot = item(jnp.maximum(back, 0), near_hops, -way)

        @pl.when(near)
        def _():
            def pass_on(which):
                to_far(which, near_owner, near_slot).wait_recv()
                to_far(which, near_owner, near_slot).start()

            by_span(near_span, pass_on)

        @pl.when(back == jnp.maximum(2 * slots * near_hops - 1, 0))
        def _():
            start_own(2)

        @pl.when(j == 4)
        def _():
            for hop in range(chips):
                a_sib(abuf, hop, 0).wait_recv()

            def own_slot(slot, carry):
                for which in range(3):
                    add(which, f, slot)
                return carry

            lax.fori_loop(0, slots, own_slot, 0)

            def early(index, carry):
                far_add(index)
                return carry

            lax.fori_loop(0, 4, early, 0)

        @pl.when(j >= 4)
        def _():
            far_add(j)

        @pl.when(near)
        def _():
            by_span(near_span, lambda which: add(which, near_owner, near_slot))

        @pl.when(is_helper & (j == 2 * slots * (far_hops - 1) + slots - 1))
        def _():
            def one(index, carry):
                add_help(0, acc_first, lax.div(index, slots), lax.rem(index, slots))
                return carry

            lax.fori_loop(0, n * slots, one, 0)
            o_first[...] = acc_first[...].astype(o_first.dtype)
            first_result.start()

        return carry

    lax.fori_loop(0, far_items, step, 0)

    out_ref[:, spans[1]] = acc[:, spans[1]].astype(out_ref.dtype)

    @pl.when(is_end)
    def _():
        first_result.wait_recv()
        out_ref[:, spans[0]] = r_first[...]
        last_result.wait_recv()
        out_ref[:, spans[2]] = r_last[...]

    @pl.when(jnp.logical_not(is_end))
    def _():
        for part in (spans[0], spans[2]):
            out_ref[:, part] = acc[:, part].astype(out_ref.dtype)

    def far_done(k, carry):
        owner, slot = f - way * lax.div(k, slots), lax.rem(k, slots)
        for which in range(3):
            to_far(which, owner, slot).wait_send()
        return carry

    lax.fori_loop(0, slots * (near_hops + 1), far_done, 0)

    def near_done(k, carry):
        owner, slot = f + way * lax.div(k, slots), lax.rem(k, slots)
        for which in range(3):
            @pl.when(sends_near(which))
            def _(which=which):
                to_near(which, owner, slot).wait_send()
        return carry

    lax.fori_loop(0, slots * (far_hops + 1), near_done, 0)

    for hop in range(1, chips):
        a_mate(abuf, hop, 0).wait_send()
    for hop in range(chips):
        a_sib(abuf, hop, 0).wait_send()

    @pl.when(is_helper)
    def _():
        for hop in range(1, chips):
            a_mate(aout, hop, 1).wait_send()
        for hop in range(chips):
            a_sib(aout, hop, 1).wait_send()
        first_result.wait_send()
        last_result.wait_send()


def per_device(mesh_shape, amplitudes, integrals, tile_ids):
    n, chips = mesh_shape["fetch"], mesh_shape["blk"] // CORES
    rows, width = amplitudes.shape
    _, slots, tile, columns = integrals.shape
    cuts = (columns * 3 // 8, columns * 7 // 8)
    first, last = cuts[0], columns - cuts[1]
    tiles = chips * CORES * width // tile
    bf16, f32, dma = jnp.bfloat16, jnp.float32, pltpu.SemaphoreType.DMA
    return pl.pallas_call(
        functools.partial(kernel, n, chips, cuts),
        out_shape=jax.ShapeDtypeStruct((rows, columns), bf16),
        in_specs=[
            pl.BlockSpec(memory_space=pltpu.SMEM),
            pl.BlockSpec(memory_space=pl.ANY),
            pl.BlockSpec(memory_space=pl.ANY),
        ],
        out_specs=pl.BlockSpec(memory_space=pltpu.VMEM),
        scratch_shapes=[
            pltpu.VMEM((tiles, rows, tile), bf16),
            pltpu.VMEM((tiles, rows, tile), bf16),
            pltpu.VMEM((n, slots, tile, columns), bf16),
            pltpu.VMEM((rows, columns), f32),
            pltpu.VMEM((rows, first), f32), pltpu.VMEM((rows, last), f32),
            pltpu.VMEM((rows, first), bf16), pltpu.VMEM((rows, last), bf16),
            pltpu.VMEM((rows, first), bf16), pltpu.VMEM((rows, last), bf16),
            dma((1 + width // tile,)),
            dma((2, chips)), dma((2, chips)),
            dma((2, chips)), dma((2, chips)),
            dma((1,)), dma((1,)),
            dma((n, slots, 3)), dma((n, slots, 3)), dma((n, slots, 3)),
            dma((2,)), dma((2,)),
        ],
        compiler_params=pltpu.CompilerParams(
            collective_id=0, has_side_effects=True, vmem_limit_bytes=56 << 20
        ),
        cost_estimate=pl.CostEstimate(
            flops=2 * rows * n * slots * tile * columns,
            bytes_accessed=4 * rows * columns, transcendentals=0,
        ),
    )(tile_ids, amplitudes, integrals)


def solution(mesh):
    placed = (
        P(("groups", "fetch"), "blk"),
        P(("groups", "blk"), "fetch", None, None),
        P(("groups", "blk"), None),
    )
    return jax.shard_map(
        functools.partial(per_device, dict(mesh.shape)),
        mesh=mesh,
        in_specs=placed,
        out_specs=P(("groups", "fetch"), "blk"),
        check_vma=False,
    )
```

```python
import functools

import jax
import jax.numpy as jnp
from jax import lax
from jax.experimental import pallas as pl
from jax.experimental.pallas import tpu as pltpu
from jax.sharding import PartitionSpec as P

CORES = 2
LAG = 3
MESH = pl.DeviceIdType.MESH


def kernel(
    n, chips, cuts,
    ids_ref, a_ref, b_ref, out_ref,
    abuf, aout, bbuf, acc, total_0, total_2, total_3, o_0, o_2, o_3, r_0, r_2, r_3,
    local_sem, a_send, a_recv, s_send, s_recv, o_send, o_recv,
    p_send, m_send, b_recv, r_send, r_recv,
):
    g = lax.axis_index("groups")
    b = lax.axis_index("blk")
    f = lax.axis_index("fetch")
    x, core = lax.div(b, CORES), lax.rem(b, CORES)
    sibling = b + 1 - 2 * core
    slots, tile, columns = b_ref.shape[1:]
    per_group = a_ref.shape[1] // tile
    spans = [slice(cuts[k], cuts[k + 1]) for k in range(4)]
    helped = {0: (total_0, o_0, r_0), 2: (total_2, o_2, r_2), 3: (total_3, o_3, r_3)}

    low = f < n // 2
    way = jnp.where(low, 1, -1)
    far_hops = jnp.where(low, n - 1 - f, f)
    near_hops = n - 1 - far_hops
    is_end = near_hops == 0
    is_helper = near_hops == 1
    has_near = near_hops > 0
    far_side = (g, b, jnp.clip(f + way, 0, n - 1))
    near_side = (g, b, jnp.clip(f - way, 0, n - 1))

    def mate(hop):
        return lax.rem(x + hop, chips) * CORES + core

    barrier = pltpu.get_barrier_semaphore()
    for hop in range(1, chips):
        pl.semaphore_signal(barrier, inc=1, device_id=(g, mate(hop), f), device_id_type=MESH)
    pl.semaphore_signal(barrier, inc=1, device_id=(g, sibling, f), device_id_type=MESH)
    pl.semaphore_signal(barrier, inc=1, device_id=far_side, device_id_type=MESH)

    @pl.when(has_near)
    def _():
        pl.semaphore_signal(barrier, inc=1, device_id=near_side, device_id_type=MESH)

    own_a = [
        pltpu.make_async_copy(
            a_ref.at[:, pl.ds(k * tile, tile)], abuf.at[b * per_group + k], local_sem.at[1 + k]
        )
        for k in range(per_group)
    ]
    own_b = pltpu.make_async_copy(b_ref.at[0], bbuf.at[f], local_sem.at[0])
    for copy in own_a:
        copy.start()
    own_b.start()
    for copy in own_a:
        copy.wait()
    pl.semaphore_wait(barrier, chips + 1 + jnp.where(has_near, 1, 0))

    def remote(src, dst, send, recv, device):
        return pltpu.make_async_remote_copy(
            src_ref=src, dst_ref=dst, send_sem=send, recv_sem=recv,
            device_id=device, device_id_type=MESH,
        )

    def b_copy(span, owner, slot, device, send, src=None):
        lanes = pl.ds(spans[span].start, spans[span].stop - spans[span].start)
        piece = bbuf.at[owner, slot, :, lanes]
        source = piece if src is None else src.at[0, slot, :, lanes]
        return remote(source, piece, send.at[owner, slot, span], b_recv.at[owner, slot, span], device)

    def to_far(span, owner, slot, src=None):
        return b_copy(span, owner, slot, far_side, p_send, src)

    def to_near(span, owner, slot, src=None):
        return b_copy(span, owner, slot, near_side, m_send, src)

    def sends_near(span):
        return has_near if span == 1 else near_hops > 1

    def a_group(buffer, owner):
        return buffer.at[pl.ds(owner * per_group, per_group)]

    def a_mate(buffer, hop, base):
        part = a_group(buffer, b)
        return remote(part, part, a_send.at[base, hop], a_recv.at[base, hop], (g, mate(hop), f))

    def a_sib(buffer, hop, base):
        part = a_group(buffer, lax.rem(x + chips - hop, chips) * CORES + core)
        return remote(part, part, s_send.at[base, hop], s_recv.at[base, hop], (g, sibling, f))

    def start_own(span):
        for slot in range(slots):
            to_far(span, f, slot, b_ref).start()

        @pl.when(sends_near(span))
        def _():
            for slot in range(slots):
                to_near(span, f, slot, b_ref).start()

    a_help = remote(a_group(abuf, b), a_group(aout, b), o_send.at[0], o_recv.at[0], far_side)

    @pl.when(is_end)
    def _():
        a_help.start()

    @pl.when(jnp.logical_not(is_end))
    def _():
        start_own(0)

    for hop in range(1, chips):
        a_mate(abuf, hop, 0).start()
    a_sib(abuf, 0, 0).start()

    @pl.when(jnp.logical_not(is_end))
    def _():
        start_own(1)

    acc[...] = jnp.zeros_like(acc)
    for total, _, _ in helped.values():
        total[...] = jnp.zeros_like(total)

    @pl.when(is_end)
    def _():
        a_help.wait_send()
        start_own(0)

    own_b.wait()

    def a_tile(buffer, owner, slot):
        name = ids_ref[0, owner * slots + slot]
        empty = lax.shift_right_arithmetic(name, 31)
        value = buffer[name - empty]
        return value * (1 + empty).astype(jnp.float32).astype(value.dtype)

    def add(span, owner, slot):
        part = spans[span]
        acc[:, part] += jnp.dot(
            a_tile(abuf, owner, slot), bbuf[owner, slot, :, part], preferred_element_type=jnp.float32
        )

    def add_help(span, owner, slot):
        total = helped[span][0]
        total[...] += jnp.dot(
            a_tile(aout, owner, slot), bbuf[owner, slot, :, spans[span]],
            preferred_element_type=jnp.float32,
        )

    def item(index, hops, direction):
        tail = index - 2 * slots * hops
        late = tail >= 0
        third = tail >= slots * hops
        within = jnp.where(third, tail - slots * hops, tail)
        span = jnp.where(third, 3, jnp.where(late, 2, lax.rem(lax.div(index, slots), 2)))
        distance = 1 + jnp.where(late, lax.div(within, slots), lax.div(index, 2 * slots))
        return span, f + direction * distance, lax.rem(index, slots)

    def by_span(span, action):
        for which in range(4):
            @pl.when(span == which)
            def _(which=which):
                action(which)

    def far_item(index):
        return item(index, far_hops, way)

    def far_add(index):
        span, owner, slot = far_item(index)

        def one(which):
            if which == 1:
                add(which, owner, slot)
            else:
                pl.when(jnp.logical_not(is_end))(lambda: add(which, owner, slot))

        by_span(span, one)

    results = {
        span: remote(out, landed, r_send.at[span], r_recv.at[span], near_side)
        for span, (_, out, landed) in helped.items()
    }

    def give_back(span):
        total, out, _ = helped[span]
        out[...] = total[...].astype(out.dtype)
        results[span].start()

    far_items = 4 * slots * far_hops
    near_items = 4 * slots * near_hops
    far_end = f + way * far_hops

    def step(j, carry):
        @pl.when(j == 3)
        def _():
            for hop in range(1, chips):
                a_mate(abuf, hop, 0).wait_recv()
                a_sib(abuf, hop, 0).start()

            @pl.when(is_helper)
            def _():
                a_help.wait_recv()
                for hop in range(1, chips):
                    a_mate(aout, hop, 1).start()
                a_sib(aout, 0, 1).start()

        @pl.when(is_helper & (j == 6))
        def _():
            for hop in range(1, chips):
                a_mate(aout, hop, 1).wait_recv()
                a_sib(aout, hop, 1).start()

        @pl.when(is_helper & (j == 7))
        def _():
            for hop in range(chips):
                a_sib(aout, hop, 1).wait_recv()

        span, owner, slot = far_item(j)

        def arrive(which):
            @pl.when(jnp.logical_not(is_end) if which != 1 else j >= 0)
            def _():
                to_near(which, owner, slot).wait_recv()

            @pl.when(sends_near(which))
            def _():
                to_near(which, owner, slot).start()

        by_span(span, arrive)

        for late in (2, 3):
            @pl.when(is_helper & (span == late) & (owner == far_end))
            def _(late=late):
                add_help(late, owner, slot)
                pl.when(slot == slots - 1)(lambda: give_back(late))

        back = j - LAG
        near = (back >= 0) & (back < near_items)
        near_span, near_owner, near_slot = item(jnp.maximum(back, 0), near_hops, -way)

        @pl.when(near)
        def _():
            def pass_on(which):
                to_far(which, near_owner, near_slot).wait_recv()
                to_far(which, near_owner, near_slot).start()

            by_span(near_span, pass_on)

        @pl.when(j == jnp.where(is_end, 4, -1))
        def _():
            for k in range(slots):
                to_far(0, f, k).wait_send()
            start_own(1)

        for late in (2, 3):
            @pl.when(j == jnp.where(is_end, 7 + late, late * slots * near_hops - 1 + LAG))
            def _(late=late):
                start_own(late)

        @pl.when(j == 4)
        def _():
            for hop in range(chips):
                a_sib(abuf, hop, 0).wait_recv()

            def early(index, carry):
                far_add(index)
                return carry

            lax.fori_loop(0, 4, early, 0)

            @pl.when(has_near)
            def _():
                for passed in range(4 - LAG):
                    add(0, f - way, passed)

        @pl.when(j >= 4)
        def _():
            far_add(j)

        @pl.when((j > 4) & (j <= 4 + slots))
        def _():
            for which in range(4):
                add(which, f, j - 5)

        @pl.when(near & (j >= 4))
        def _():
            by_span(near_span, lambda which: add(which, near_owner, near_slot))

        def help_all(span, owners):
            def one(index, carry):
                add_help(span, lax.div(index, slots) + owners, lax.rem(index, slots))
                return carry

            return one

        @pl.when(is_helper & (j == 2 * slots * (far_hops - 1) + slots - 1))
        def _():
            lax.fori_loop(0, n * slots, help_all(0, 0), 0)
            give_back(0)

        for late in (2, 3):
            @pl.when(is_helper & (j == slots * (late * far_hops + far_hops - 1) - 1))
            def _(late=late):
                skip = jnp.where(far_end == 0, 1, 0)
                lax.fori_loop(0, (n - 1) * slots, help_all(late, skip), 0)

        @pl.when(j == 2 * slots * far_hops)
        def _():
            for part in (spans[0], spans[1]):
                out_ref[:, part] = acc[:, part].astype(out_ref.dtype)

        return carry

    lax.fori_loop(0, far_items, step, 0)

    @pl.when(is_end)
    def _():
        for span, (_, _, landed) in helped.items():
            results[span].wait_recv()
            out_ref[:, spans[span]] = landed[...]

    @pl.when(jnp.logical_not(is_end))
    def _():
        for part in (spans[2], spans[3]):
            out_ref[:, part] = acc[:, part].astype(out_ref.dtype)

    def far_done(k, carry):
        owner, slot = f - way * lax.div(k, slots), lax.rem(k, slots)
        pl.when(jnp.logical_not(is_end))(lambda: to_far(0, owner, slot).wait_send())
        for which in range(1, 4):
            to_far(which, owner, slot).wait_send()
        return carry

    lax.fori_loop(0, slots * (near_hops + 1), far_done, 0)

    def near_done(k, carry):
        owner, slot = f + way * lax.div(k, slots), lax.rem(k, slots)
        for which in range(4):
            @pl.when(sends_near(which))
            def _(which=which):
                to_near(which, owner, slot).wait_send()
        return carry

    lax.fori_loop(0, slots * (far_hops + 1), near_done, 0)

    for hop in range(1, chips):
        a_mate(abuf, hop, 0).wait_send()
    for hop in range(chips):
        a_sib(abuf, hop, 0).wait_send()

    @pl.when(is_helper)
    def _():
        for hop in range(1, chips):
            a_mate(aout, hop, 1).wait_send()
        for hop in range(chips):
            a_sib(aout, hop, 1).wait_send()
        for result in results.values():
            result.wait_send()


def per_device(mesh_shape, amplitudes, integrals, tile_ids):
    n, chips = mesh_shape["fetch"], mesh_shape["blk"] // CORES
    rows, width = amplitudes.shape
    _, slots, tile, columns = integrals.shape
    cuts = tuple(columns * eighths // 8 for eighths in (0, 2, 6, 7, 8))
    helped = [cuts[k + 1] - cuts[k] for k in (0, 2, 3)]
    tiles = chips * CORES * width // tile
    bf16, f32, dma = jnp.bfloat16, jnp.float32, pltpu.SemaphoreType.DMA
    return pl.pallas_call(
        functools.partial(kernel, n, chips, cuts),
        out_shape=jax.ShapeDtypeStruct((rows, columns), bf16),
        in_specs=[
            pl.BlockSpec(memory_space=pltpu.SMEM),
            pl.BlockSpec(memory_space=pl.ANY),
            pl.BlockSpec(memory_space=pl.ANY),
        ],
        out_specs=pl.BlockSpec(memory_space=pltpu.VMEM),
        scratch_shapes=[
            pltpu.VMEM((tiles, rows, tile), bf16),
            pltpu.VMEM((tiles, rows, tile), bf16),
            pltpu.VMEM((n, slots, tile, columns), bf16),
            pltpu.VMEM((rows, columns), f32),
            *[pltpu.VMEM((rows, size), kind) for kind in (f32, bf16, bf16) for size in helped],
            dma((1 + width // tile,)),
            dma((2, chips)), dma((2, chips)),
            dma((2, chips)), dma((2, chips)),
            dma((1,)), dma((1,)),
            dma((n, slots, 4)), dma((n, slots, 4)), dma((n, slots, 4)),
            dma((4,)), dma((4,)),
        ],
        compiler_params=pltpu.CompilerParams(
            collective_id=0, has_side_effects=True, vmem_limit_bytes=56 << 20
        ),
        cost_estimate=pl.CostEstimate(
            flops=2 * rows * n * slots * tile * columns,
            bytes_accessed=4 * rows * columns, transcendentals=0,
        ),
    )(tile_ids, amplitudes, integrals)


def solution(mesh):
    placed = (
        P(("groups", "fetch"), "blk"),
        P(("groups", "blk"), "fetch", None, None),
        P(("groups", "blk"), None),
    )
    return jax.shard_map(
        functools.partial(per_device, dict(mesh.shape)),
        mesh=mesh,
        in_specs=placed,
        out_specs=P(("groups", "fetch"), "blk"),
        check_vma=False,
    )
```

```python
import functools

import jax
import jax.numpy as jnp
from jax import lax
from jax.experimental import pallas as pl
from jax.experimental.pallas import tpu as pltpu
from jax.sharding import PartitionSpec as P

CORES = 2
LAG = 3
MESH = pl.DeviceIdType.MESH


def kernel(
    n, chips, cuts,
    ids_ref, a_ref, b_ref, out_ref,
    abuf, aout, bbuf, acc, total_0, total_2, total_3, o_0, o_2, o_3, r_0, r_2, r_3,
    local_sem, a_send, a_recv, s_send, s_recv, o_send, o_recv,
    p_send, m_send, b_recv, r_send, r_recv,
):
    g = lax.axis_index("groups")
    b = lax.axis_index("blk")
    f = lax.axis_index("fetch")
    x, core = lax.div(b, CORES), lax.rem(b, CORES)
    sibling = b + 1 - 2 * core
    slots, tile, columns = b_ref.shape[1:]
    per_group = a_ref.shape[1] // tile
    spans = [slice(cuts[k], cuts[k + 1]) for k in range(4)]
    helped = {0: (total_0, o_0, r_0), 2: (total_2, o_2, r_2), 3: (total_3, o_3, r_3)}

    low = f < n // 2
    way = jnp.where(low, 1, -1)
    far_hops = jnp.where(low, n - 1 - f, f)
    near_hops = n - 1 - far_hops
    is_end = near_hops == 0
    is_helper = near_hops == 1
    has_near = near_hops > 0
    far_side = (g, b, jnp.clip(f + way, 0, n - 1))
    near_side = (g, b, jnp.clip(f - way, 0, n - 1))

    def mate(hop):
        return lax.rem(x + hop, chips) * CORES + core

    barrier = pltpu.get_barrier_semaphore()
    for hop in range(1, chips):
        pl.semaphore_signal(barrier, inc=1, device_id=(g, mate(hop), f), device_id_type=MESH)
    pl.semaphore_signal(barrier, inc=1, device_id=(g, sibling, f), device_id_type=MESH)
    pl.semaphore_signal(barrier, inc=1, device_id=far_side, device_id_type=MESH)

    @pl.when(has_near)
    def _():
        pl.semaphore_signal(barrier, inc=1, device_id=near_side, device_id_type=MESH)

    own_a = [
        pltpu.make_async_copy(
            a_ref.at[:, pl.ds(k * tile, tile)], abuf.at[b * per_group + k], local_sem.at[1 + k]
        )
        for k in range(per_group)
    ]
    own_b = pltpu.make_async_copy(b_ref.at[0], bbuf.at[f], local_sem.at[0])
    for copy in own_a:
        copy.start()
    own_b.start()
    for copy in own_a:
        copy.wait()
    pl.semaphore_wait(barrier, chips + 1 + jnp.where(has_near, 1, 0))

    def remote(src, dst, send, recv, device):
        return pltpu.make_async_remote_copy(
            src_ref=src, dst_ref=dst, send_sem=send, recv_sem=recv,
            device_id=device, device_id_type=MESH,
        )

    def b_copy(span, owner, slot, device, send, src=None):
        lanes = pl.ds(spans[span].start, spans[span].stop - spans[span].start)
        piece = bbuf.at[owner, slot, :, lanes]
        source = piece if src is None else src.at[0, slot, :, lanes]
        return remote(source, piece, send.at[owner, slot, span], b_recv.at[owner, slot, span], device)

    def to_far(span, owner, slot, src=None):
        return b_copy(span, owner, slot, far_side, p_send, src)

    def to_near(span, owner, slot, src=None):
        return b_copy(span, owner, slot, near_side, m_send, src)

    def sends_near(span):
        return has_near if span == 1 else near_hops > 1

    def a_group(buffer, owner):
        return buffer.at[pl.ds(owner * per_group, per_group)]

    def a_mate(buffer, hop, base):
        part = a_group(buffer, b)
        return remote(part, part, a_send.at[base, hop], a_recv.at[base, hop], (g, mate(hop), f))

    def a_sib(buffer, hop, base):
        part = a_group(buffer, lax.rem(x + chips - hop, chips) * CORES + core)
        return remote(part, part, s_send.at[base, hop], s_recv.at[base, hop], (g, sibling, f))

    def start_own(span):
        for slot in range(slots):
            to_far(span, f, slot, b_ref).start()

        @pl.when(sends_near(span))
        def _():
            for slot in range(slots):
                to_near(span, f, slot, b_ref).start()

    a_help = remote(a_group(abuf, b), a_group(aout, b), o_send.at[0], o_recv.at[0], far_side)

    @pl.when(is_end)
    def _():
        a_help.start()

    @pl.when(jnp.logical_not(is_end))
    def _():
        start_own(0)

    for hop in range(1, chips):
        a_mate(abuf, hop, 0).start()
    a_sib(abuf, 0, 0).start()

    @pl.when(jnp.logical_not(is_end))
    def _():
        start_own(1)

    acc[...] = jnp.zeros_like(acc)
    for total, _, _ in helped.values():
        total[...] = jnp.zeros_like(total)

    @pl.when(is_end)
    def _():
        a_help.wait_send()
        start_own(0)

    own_b.wait()

    def a_tile(buffer, owner, slot):
        name = ids_ref[0, owner * slots + slot]
        empty = lax.shift_right_arithmetic(name, 31)
        value = buffer[name - empty]
        return value * (1 + empty).astype(jnp.float32).astype(value.dtype)

    def add(span, owner, slot):
        part = spans[span]
        acc[:, part] += jnp.dot(
            a_tile(abuf, owner, slot), bbuf[owner, slot, :, part], preferred_element_type=jnp.float32
        )

    def add_help(span, owner, slot):
        total = helped[span][0]
        total[...] += jnp.dot(
            a_tile(aout, owner, slot), bbuf[owner, slot, :, spans[span]],
            preferred_element_type=jnp.float32,
        )

    def item(index, hops, direction):
        tail = index - 2 * slots * hops
        late = tail >= 0
        third = tail >= slots * hops
        within = jnp.where(third, tail - slots * hops, tail)
        span = jnp.where(third, 3, jnp.where(late, 2, lax.rem(lax.div(index, slots), 2)))
        distance = 1 + jnp.where(late, lax.div(within, slots), lax.div(index, 2 * slots))
        return span, f + direction * distance, lax.rem(index, slots)

    def by_span(span, action):
        for which in range(4):
            @pl.when(span == which)
            def _(which=which):
                action(which)

    def far_item(index):
        return item(index, far_hops, way)

    def far_add(index):
        span, owner, slot = far_item(index)

        def one(which):
            if which == 1:
                add(which, owner, slot)
            else:
                pl.when(jnp.logical_not(is_end))(lambda: add(which, owner, slot))

        by_span(span, one)

    results = {
        span: remote(out, landed, r_send.at[span], r_recv.at[span], near_side)
        for span, (_, out, landed) in helped.items()
    }

    def give_back(span):
        total, out, _ = helped[span]
        out[...] = total[...].astype(out.dtype)
        results[span].start()

    far_items = 4 * slots * far_hops
    near_items = 4 * slots * near_hops
    far_end = f + way * far_hops

    def step(j, carry):
        @pl.when(j == 3)
        def _():
            for hop in range(1, chips):
                a_mate(abuf, hop, 0).wait_recv()
                a_sib(abuf, hop, 0).start()

            @pl.when(is_helper)
            def _():
                a_help.wait_recv()
                for hop in range(1, chips):
                    a_mate(aout, hop, 1).start()
                a_sib(aout, 0, 1).start()

        @pl.when(is_helper & (j == 6))
        def _():
            for hop in range(1, chips):
                a_mate(aout, hop, 1).wait_recv()
                a_sib(aout, hop, 1).start()

        @pl.when(is_helper & (j == 7))
        def _():
            for hop in range(chips):
                a_sib(aout, hop, 1).wait_recv()

        span, owner, slot = far_item(j)

        def arrive(which):
            @pl.when(jnp.logical_not(is_end) if which != 1 else j >= 0)
            def _():
                to_near(which, owner, slot).wait_recv()

            @pl.when(sends_near(which))
            def _():
                to_near(which, owner, slot).start()

        by_span(span, arrive)

        for late in (2, 3):
            @pl.when(is_helper & (span == late) & (owner == far_end))
            def _(late=late):
                add_help(late, owner, slot)
                pl.when(slot == slots - 1)(lambda: give_back(late))

        back = j - LAG
        near = (back >= 0) & (back < near_items)
        near_span, near_owner, near_slot = item(jnp.maximum(back, 0), near_hops, -way)

        @pl.when(near)
        def _():
            def pass_on(which):
                to_far(which, near_owner, near_slot).wait_recv()
                to_far(which, near_owner, near_slot).start()

            by_span(near_span, pass_on)

        @pl.when(j == jnp.where(is_end, 4, -1))
        def _():
            for k in range(slots):
                to_far(0, f, k).wait_send()
            start_own(1)

        for late in (2, 3):
            @pl.when(j == jnp.where(is_end, 7 + late, late * slots * near_hops + LAG))
            def _(late=late):
                start_own(late)

        @pl.when(j == 4)
        def _():
            for hop in range(chips):
                a_sib(abuf, hop, 0).wait_recv()

            def early(index, carry):
                far_add(index)
                return carry

            lax.fori_loop(0, 4, early, 0)

            @pl.when(has_near)
            def _():
                for passed in range(4 - LAG):
                    add(0, f - way, passed)

        @pl.when(j >= 4)
        def _():
            far_add(j)

        @pl.when((j > 4) & (j <= 4 + slots))
        def _():
            for which in range(4):
                add(which, f, j - 5)

        @pl.when(near & (j >= 4))
        def _():
            by_span(near_span, lambda which: add(which, near_owner, near_slot))

        def help_all(span, owners):
            def one(index, carry):
                add_help(span, lax.div(index, slots) + owners, lax.rem(index, slots))
                return carry

            return one

        @pl.when(is_helper & (j == 2 * slots * (far_hops - 1) + slots - 1))
        def _():
            lax.fori_loop(0, n * slots, help_all(0, 0), 0)
            give_back(0)

        for late in (2, 3):
            @pl.when(is_helper & (j == slots * (late * far_hops + far_hops - 1) - 1))
            def _(late=late):
                skip = jnp.where(far_end == 0, 1, 0)
                lax.fori_loop(0, (n - 1) * slots, help_all(late, skip), 0)

        @pl.when(j == 2 * slots * far_hops)
        def _():
            for part in (spans[0], spans[1]):
                out_ref[:, part] = acc[:, part].astype(out_ref.dtype)

        return carry

    lax.fori_loop(0, far_items, step, 0)

    @pl.when(is_end)
    def _():
        for span, (_, _, landed) in helped.items():
            results[span].wait_recv()
            out_ref[:, spans[span]] = landed[...]

    @pl.when(jnp.logical_not(is_end))
    def _():
        for part in (spans[2], spans[3]):
            out_ref[:, part] = acc[:, part].astype(out_ref.dtype)

    def far_done(k, carry):
        owner, slot = f - way * lax.div(k, slots), lax.rem(k, slots)
        pl.when(jnp.logical_not(is_end))(lambda: to_far(0, owner, slot).wait_send())
        for which in range(1, 4):
            to_far(which, owner, slot).wait_send()
        return carry

    lax.fori_loop(0, slots * (near_hops + 1), far_done, 0)

    def near_done(k, carry):
        owner, slot = f + way * lax.div(k, slots), lax.rem(k, slots)
        for which in range(4):
            @pl.when(sends_near(which))
            def _(which=which):
                to_near(which, owner, slot).wait_send()
        return carry

    lax.fori_loop(0, slots * (far_hops + 1), near_done, 0)

    for hop in range(1, chips):
        a_mate(abuf, hop, 0).wait_send()
    for hop in range(chips):
        a_sib(abuf, hop, 0).wait_send()

    @pl.when(is_helper)
    def _():
        for hop in range(1, chips):
            a_mate(aout, hop, 1).wait_send()
        for hop in range(chips):
            a_sib(aout, hop, 1).wait_send()
        for result in results.values():
            result.wait_send()


def per_device(mesh_shape, amplitudes, integrals, tile_ids):
    n, chips = mesh_shape["fetch"], mesh_shape["blk"] // CORES
    rows, width = amplitudes.shape
    _, slots, tile, columns = integrals.shape
    cuts = tuple(columns * eighths // 8 for eighths in (0, 2, 6, 7, 8))
    helped = [cuts[k + 1] - cuts[k] for k in (0, 2, 3)]
    tiles = chips * CORES * width // tile
    bf16, f32, dma = jnp.bfloat16, jnp.float32, pltpu.SemaphoreType.DMA
    return pl.pallas_call(
        functools.partial(kernel, n, chips, cuts),
        out_shape=jax.ShapeDtypeStruct((rows, columns), bf16),
        in_specs=[
            pl.BlockSpec(memory_space=pltpu.SMEM),
            pl.BlockSpec(memory_space=pl.ANY),
            pl.BlockSpec(memory_space=pl.ANY),
        ],
        out_specs=pl.BlockSpec(memory_space=pltpu.VMEM),
        scratch_shapes=[
            pltpu.VMEM((tiles, rows, tile), bf16),
            pltpu.VMEM((tiles, rows, tile), bf16),
            pltpu.VMEM((n, slots, tile, columns), bf16),
            pltpu.VMEM((rows, columns), f32),
            *[pltpu.VMEM((rows, size), kind) for kind in (f32, bf16, bf16) for size in helped],
            dma((1 + width // tile,)),
            dma((2, chips)), dma((2, chips)),
            dma((2, chips)), dma((2, chips)),
            dma((1,)), dma((1,)),
            dma((n, slots, 4)), dma((n, slots, 4)), dma((n, slots, 4)),
            dma((4,)), dma((4,)),
        ],
        compiler_params=pltpu.CompilerParams(
            collective_id=0, has_side_effects=True, vmem_limit_bytes=56 << 20
        ),
        cost_estimate=pl.CostEstimate(
            flops=2 * rows * n * slots * tile * columns,
            bytes_accessed=4 * rows * columns, transcendentals=0,
        ),
    )(tile_ids, amplitudes, integrals)


def solution(mesh):
    placed = (
        P(("groups", "fetch"), "blk"),
        P(("groups", "blk"), "fetch", None, None),
        P(("groups", "blk"), None),
    )
    return jax.shard_map(
        functools.partial(per_device, dict(mesh.shape)),
        mesh=mesh,
        in_specs=placed,
        out_specs=P(("groups", "fetch"), "blk"),
        check_vma=False,
    )
```
